128 devices in a mesh: dp: 16 (over x_lo, y, core), tensor: 8 (over z, x_hi).
Axes of the slice: x: 4 (x_hi: 2, x_lo: 2; x = x_hi * 2 + x_lo), y: 4, z: 4, core: 2. Of those that a mesh axis runs over, the one named last changes fastest.
Arguments:
- q_latent: bfloat16 [1024, 64, 576], P(('dp', 'tensor')), may hold values from -4 to 4
- kv_cache: bfloat16 [1024, 512, 576], P(('dp', 'tensor')), may hold values from -4 to 4
- new_latent: bfloat16 [1024, 576], P(('dp', 'tensor')), may hold values from -4 to 4
- cache_len: int32 [1024], P(('dp', 'tensor')), may hold values from 2 to 512, as said below
- residual: bfloat16 [1024, 4096], P('dp'), may hold values from -3 to 3
- w_uv: bfloat16 [64, 512, 128], P('tensor'), may hold values from -1 to 1
- w_out: bfloat16 [8192, 4096], P('tensor'), may hold values from -0.0625 to 0.0625
- norm_gain: float32 [4096], replicated, may hold values from 0.1 to 1.9
- routes: int32 [1024, 8], P('dp'), may hold values from 0 to 31, all different within a row; in each aligned block of 64 rows (0 to 63, 64 to 127, ...) at most 32 rows name the same one
- route_weight: float32 [1024, 8], P('dp'), may hold values from 0.05 to 0.5
- placement: int32 [32], replicated, may hold values from 0 to 47, as said below
- w_gate: bfloat16 [48, 4096, 1024], P('dp', None, 'tensor'), may hold values from -0.09375 to 0.09375
- w_up: bfloat16 [48, 4096, 1024], P('dp', None, 'tensor'), may hold values from -0.09375 to 0.09375
- w_down: bfloat16 [48, 1024, 4096], P('dp', 'tensor'), may hold values from -0.1875 to 0.1875
Outputs:
- layer_out: bfloat16 [1024, 4096], P('dp', 'tensor')
The draws below stay inside these ranges and needn't reach their ends.
Inputs may be any that keep to these rules, and one draw needn't show every extreme that they name: `cache_len`: in every draw one row's length is exactly 512. `routes`: A row names 8 different experts; in each aligned block of 64 rows (the rows of one index of dp) no expert is named by more than 32 rows. `placement`: distinct slots; slot s belongs to index s // 3 of dp; the 3 slots of one index of dp (never the last index) serve no expert; slot 47 always serves one; some index of dp serves 3 experts.
All inputs are finite; a program needn't handle non-finite values.
Results may differ from the reference program's by a relative error of at most 0.024.
Values may be sent and summed in bfloat16 or wider, within the bound.
No kernel may reach another device: no remote copies, remote signals or barrier semaphores. Data moves between devices by JAX's collectives and lax.ppermute only.
A program may use at most 128 MiB of HBM per device.

```python
import math
import jax
import jax.numpy as jnp
import numpy as np
from jax import lax

D = 4096
HEADS = 64
LATENT = 512
ROPE = 64
V_HEAD = 128
FF = 1024
TOP = 8
SLOT_DEV = 3
R = 64
LEN = 512
ROWS = 1024
KV = 576
EXPERTS = 32
SLOTS = 48
CAP = 32
N_DP = 16
N_TENSOR = 8


def draw_q_latent(key, part):
    key = jax.random.fold_in(key, 3)
    values = jnp.clip(jax.random.normal(key, (ROWS, HEADS, KV), jnp.float32), -4.0, 4.0)
    return values.astype(jnp.bfloat16)


def draw_kv_cache(key, part):
    key = jax.random.fold_in(key, 4)
    values = jnp.clip(jax.random.normal(key, (ROWS, LEN, KV), jnp.float32), -4.0, 4.0)
    return values.astype(jnp.bfloat16)


def draw_cache_len(key, part):
    key = jax.random.fold_in(key, 5)
    key_first, key_second, key_third = jax.random.split(key, 3)
    ceiling = jax.random.randint(key_first, (ROWS // R,), LEN // 4, LEN + 1)
    uniform_draw = jax.random.randint(key_second, (ROWS,), 0, LEN + 1)
    row_limit = jnp.repeat(ceiling, R)
    lengths = 2 + uniform_draw * (row_limit - 2) // LEN
    longest = jax.random.randint(key_third, (), 0, ROWS)
    lengths = jnp.where(jnp.arange(ROWS) == longest, LEN, lengths)
    return lengths.astype(jnp.int32)


def draw_placement(key, part):
    key = jax.random.fold_in(key, 7)
    key_lost, key_pick, key_order = jax.random.split(key, 3)
    owners = SLOTS // SLOT_DEV
    lost_owner = jax.random.randint(key_lost, (), 0, owners - 1)
    picked = jax.random.permutation(key_pick, SLOTS - SLOT_DEV - 1)[:EXPERTS - 1].astype(jnp.int32)
    picked = jnp.where(picked >= lost_owner * SLOT_DEV, picked + SLOT_DEV, picked)
    chosen = jnp.concatenate([picked, jnp.full((1,), SLOTS - 1, jnp.int32)])
    new_order = jax.random.permutation(key_order, EXPERTS)
    return chosen[new_order].astype(jnp.int32)


def steps_of(rng, shape, cuts, least, largest):
    loudness, own = 1.0, jax.random.fold_in(rng, 6)
    for axis_at, blocks in cuts:
        steps = jnp.exp(jax.random.uniform(jax.random.fold_in(own, axis_at), (blocks,), jnp.float32, least / len(cuts), largest / len(cuts)))
        loudness = loudness * jnp.repeat(steps, shape[axis_at] // blocks).reshape([-1 if axis == axis_at else 1 for axis in range(len(shape))])
    return loudness


def deal_out(key, own, number, rows, count, top, most, slope):
    order = jax.random.permutation(key, count)
    crowded, usual = portions_of(count, rows * top, most, slope, True), portions_of(count, rows * top, most, slope, False)
    places = jnp.arange(count)

    def named(sizes, turn):
        used = int((sizes > 0).sum())
        fixed = max(1, used // 4)
        moved = fixed + (places - fixed + turn * (used - fixed)) % max(1, count - fixed)
        return jnp.zeros((count,), jnp.int32).at[order[jnp.where(places < fixed, places, moved)]].set(jnp.asarray(sizes, jnp.int32))

    sizes = jnp.where(number % 4 == 0, named(crowded, number // 4), named(usual, number - number // 4 - 1))
    mixed = jax.random.permutation(jax.random.fold_in(own, 3), count)
    source_of, taker = mixed[0:count // 2 * 2:2], mixed[1:count // 2 * 2:2]
    margin = jnp.minimum(sizes[source_of] - 1, most - sizes[taker]) // 2
    margin = jnp.where((source_of == order[0]) | (taker == order[0]) | (sizes[taker] == 0), 0, jnp.maximum(margin, 0))
    moved = jax.random.randint(jax.random.fold_in(own, 4), (count // 2,), 0, 1 << 20) % (margin + 1)
    sizes = sizes.at[source_of].add(-moved).at[taker].add(moved)
    items = jnp.searchsorted(jnp.cumsum(sizes), jnp.arange(rows * top), side="right").astype(jnp.int32)
    grid = items.reshape(top, rows).T
    grid = grid[jax.random.permutation(jax.random.fold_in(own, 1), rows)]
    turn = jax.random.randint(jax.random.fold_in(own, 2), (rows, 1), 0, top)
    return jnp.take_along_axis(grid, (jnp.arange(top)[None, :] + turn) % top, axis=1)


def portions_of(amount, total, bound, slope, full):
    portions = [(1 << 20) // math.isqrt(standing ** slope) + 1 for standing in range(1, amount + 1)]
    largest = bound if full else min(bound, max(-(-total // amount), total * portions[0] // sum(portions)))
    least = 1 if total - largest >= amount - 1 else 0
    given, surplus = [largest] + [least] * (amount - 1), total - largest - least * (amount - 1)
    while surplus > 0:
        free = [i for i in range(1, amount) if given[i] < largest] or [i for i in range(1, amount) if given[i] < bound]
        pool, budget = sum([portions[i] for i in free]), surplus
        for i in free:
            extra = min(bound - given[i], max(1, budget * portions[i] // pool), surplus)
            given[i] = given[i] + extra
            surplus = surplus - extra
    return np.array(given)


def scatter_about(own_key, extent, width, most, cuts=(), held_as=jnp.bfloat16):
    values = jax.random.normal(own_key, extent, jnp.float32) * width
    if len(cuts) > 0:
        values = steps_of(own_key, extent, cuts, -0.22, 0.18) * values
    return jnp.clip(values, min=-most, max=most).astype(held_as)


def setup_inputs(seed: int = 0) -> dict:
    seeds = jax.random.split(jax.random.key(seed), 15)
    q_latent = draw_q_latent(jax.random.fold_in(seeds[14], 71), 0)
    kv_cache = draw_kv_cache(jax.random.fold_in(seeds[14], 71), 0)
    new_latent = scatter_about(seeds[2], (ROWS, KV), 1.0, 4.0, ((0, 128),))
    cache_len = draw_cache_len(jax.random.fold_in(seeds[14], 71), 0)
    residual = scatter_about(seeds[4], (ROWS, D), 0.5, 3.0, ((0, 16),))
    w_uv = scatter_about(seeds[5], (HEADS, LATENT, V_HEAD), (LATENT // 16) ** -0.5, 1.0, ((0, 8),))
    w_out = scatter_about(seeds[6], (HEADS * V_HEAD, D), (HEADS * V_HEAD) ** -0.5, 0.0625, ((0, 8),))
    norm_gain = jnp.clip(1.0 + 0.18 * jax.random.normal(seeds[7], (D,), jnp.float32), 0.1, 1.9)
    routes_keys = jax.random.split(jax.random.fold_in(seeds[8], 1), ROWS // R)
    routes_turns = jax.random.permutation(jax.random.fold_in(seeds[8], 3), ROWS // R)
    routes = jax.vmap(lambda own, number: deal_out(jax.random.fold_in(seeds[8], 2), own, number, R, EXPERTS, TOP, CAP, 2))(routes_keys, routes_turns).reshape((ROWS, TOP))
    route_weight = jnp.clip(jnp.exp(math.log(0.5) - 2.3025851 * jax.random.uniform(seeds[9], (ROWS, TOP), jnp.float32) ** steps_of(seeds[9], (ROWS, TOP), ((0, 16),), -0.2, 0.2)), 0.05, 0.5)
    placement = draw_placement(jax.random.fold_in(seeds[14], 71), 0)
    w_gate = scatter_about(seeds[11], (SLOTS, D, FF), D ** -0.5, 0.09375, ((0, 16), (2, 8)))
    w_up = scatter_about(seeds[12], (SLOTS, D, FF), D ** -0.5, 0.09375, ((0, 16), (2, 8)))
    w_down = scatter_about(seeds[13], (SLOTS, FF, D), FF ** -0.5, 0.1875, ((0, 16), (1, 8)))
    return dict(q_latent=q_latent, kv_cache=kv_cache, new_latent=new_latent, cache_len=cache_len, residual=residual, w_uv=w_uv, w_out=w_out, norm_gain=norm_gain, routes=routes, route_weight=route_weight, placement=placement, w_gate=w_gate, w_up=w_up, w_down=w_down)


NEG = -1e+30

def attend(pieces):
    queries, cached, newest, lengths = pieces
    scale_factor = (V_HEAD + ROPE) ** (-0.5)
    query_f = queries.astype(jnp.float32)
    cache_f = cached.astype(jnp.float32)
    newest_f = newest.astype(jnp.float32)
    scores = jnp.einsum('bhk,bpk->bhp', query_f, cache_f) * scale_factor
    own_score = jnp.einsum('bhk,bk->bh', query_f, newest_f) * scale_factor
    position = jnp.arange(LEN, dtype=jnp.int32)
    in_range = position[None, None, :] < lengths[:, None, None]
    highest = jnp.maximum(lax.optimization_barrier(jnp.max(jnp.where(in_range, scores, NEG), axis=2)), own_score)
    weights = jnp.where(in_range, jnp.exp(scores - highest[..., None]), 0.0)
    own_weight = jnp.exp(own_score - highest)
    denominator = lax.optimization_barrier(jnp.sum(weights, axis=2)) + own_weight
    summed = jnp.einsum('bhp,bpl->bhl', weights, cache_f[:, :, :LATENT]) + own_weight[..., None] * newest_f[:, None, :LATENT]
    return (summed / denominator[..., None]).astype(jnp.bfloat16)

def reference(q_latent, kv_cache, new_latent, cache_len, residual, w_uv, w_out, norm_gain, routes, route_weight, placement, w_gate, w_up, w_down):
    block_rows = R // N_TENSOR
    block_count = ROWS // block_rows
    latent = lax.map(attend, (q_latent.reshape(block_count, block_rows, HEADS, KV), kv_cache.reshape(block_count, block_rows, LEN, KV), new_latent.reshape(block_count, block_rows, KV), cache_len.reshape(block_count, block_rows)))
    latent = latent.reshape(ROWS, HEADS, LATENT)
    heads_out = jnp.einsum('rhl,hlv->rhv', latent.astype(jnp.float32), w_uv.astype(jnp.float32)).astype(jnp.bfloat16)
    attn_out = jnp.dot(heads_out.reshape(ROWS, HEADS * V_HEAD), w_out, preferred_element_type=jnp.float32).astype(jnp.bfloat16)
    hidden = (residual.astype(jnp.float32) + lax.optimization_barrier(attn_out).astype(jnp.float32)).astype(jnp.bfloat16)
    hidden_f = lax.optimization_barrier(hidden).astype(jnp.float32)
    normed = (hidden_f * lax.rsqrt(lax.optimization_barrier(jnp.mean(hidden_f * hidden_f, axis=1, keepdims=True)) + 1e-06) * norm_gain).astype(jnp.bfloat16)
    assign_count = ROWS * TOP
    expert_of = routes.reshape(assign_count)
    onehot = (expert_of[:, None] == jnp.arange(EXPERTS, dtype=jnp.int32)[None, :]).astype(jnp.int32)
    rank_in = lax.optimization_barrier(jnp.sum((jnp.cumsum(onehot, axis=0) - onehot) * onehot, axis=1))
    per_expert = N_DP * CAP
    bucket = expert_of * per_expert + rank_in
    row_of = jnp.arange(assign_count, dtype=jnp.int32) // TOP
    source = jnp.zeros((EXPERTS * per_expert,), jnp.int32).at[bucket].set(row_of)
    inputs = normed[source].reshape(EXPERTS, per_expert, D)
    group_size = FF // N_TENSOR

    def expert_run(expert_args):
        expert_rows, slot_index = expert_args
        gate_pre = jnp.dot(expert_rows, w_gate[slot_index], preferred_element_type=jnp.float32)
        up_pre = jnp.dot(expert_rows, w_up[slot_index], preferred_element_type=jnp.float32)
        inner_act = (jax.nn.silu(gate_pre) * up_pre).astype(jnp.bfloat16)
        group_terms = jnp.einsum('ntf,tfd->ntd', inner_act.reshape(per_expert, N_TENSOR, group_size).astype(jnp.float32), w_down[slot_index].reshape(N_TENSOR, group_size, D).astype(jnp.float32))
        rounded = lax.optimization_barrier(group_terms.astype(jnp.bfloat16))
        return lax.optimization_barrier(jnp.sum(rounded.astype(jnp.float32), axis=1)).astype(jnp.bfloat16)
    outputs = lax.map(expert_run, (inputs, placement))
    picked = outputs.reshape(EXPERTS * per_expert, D)[bucket].reshape(ROWS, TOP, D).astype(jnp.float32)
    mixture = lax.optimization_barrier(jnp.sum(route_weight[..., None] * picked, axis=1))
    return (hidden_f + mixture).astype(jnp.bfloat16)
```

```python
import jax
import jax.numpy as jnp
from jax import lax
from jax.experimental import pallas as pl
from jax.experimental.pallas import tpu as pltpu
from jax.sharding import Mesh, PartitionSpec as P

LATENT = 512
ROPE = 64
V_HEAD = 128
NEG = -1e30

DP = ("xl", "y", "c")
TN = ("z", "xh")
CHIPS = ("xl", "y", "z", "xh")
SWAP = [(0, 1), (1, 0)]


def attend(q_latent, kv_cache, new_latent, cache_len):
    scale_factor = (V_HEAD + ROPE) ** (-0.5)
    scores = (
        jnp.einsum("bhk,bpk->bhp", q_latent, kv_cache, preferred_element_type=jnp.float32)
        * scale_factor
    )
    own_score = (
        jnp.einsum("bhk,bk->bh", q_latent, new_latent, preferred_element_type=jnp.float32)
        * scale_factor
    )
    position = jnp.arange(kv_cache.shape[1], dtype=jnp.int32)
    in_range = position[None, None, :] < cache_len[:, None, None]
    highest = jnp.maximum(jnp.max(jnp.where(in_range, scores, NEG), axis=2), own_score)
    weights = jnp.where(in_range, jnp.exp(scores - highest[..., None]), 0.0)
    own_weight = jnp.exp(own_score - highest)
    denominator = jnp.sum(weights, axis=2) + own_weight
    summed = jnp.einsum("bhp,bpl->bhl", weights, kv_cache[:, :, :LATENT].astype(jnp.float32))
    summed = summed + own_weight[..., None] * new_latent[:, None, :LATENT].astype(jnp.float32)
    return (summed / denominator[..., None]).astype(jnp.bfloat16)


def experts_kernel(x_ref, mix_ref, wg_ref, wu_ref, wd_ref, out_ref):
    x = x_ref[...]
    mix = mix_ref[...]
    parts = []
    for s in range(3):
        both = jnp.concatenate([wg_ref[s], wu_ref[s]], axis=1)
        pre = jnp.dot(x, both, preferred_element_type=jnp.float32)
        gate, up = pre[:, :128], pre[:, 128:]
        act = gate / (1.0 + jnp.exp(-gate)) * up * mix[:, s : s + 1]
        parts.append(act.astype(jnp.bfloat16))
    inner = jnp.concatenate(parts, axis=1)
    blocks = out_ref.shape[0]
    for t in range(8):
        w = wd_ref[:, t * 512 : (t + 1) * 512]
        piece = jnp.dot(inner, w, preferred_element_type=jnp.float32).astype(jnp.bfloat16)
        out_ref[:, t] = piece.reshape(blocks, 64, 512)


def experts(x, mix, w_gate, w_up, w_down):
    rows = x.shape[0]
    tile = 256
    return pl.pallas_call(
        experts_kernel,
        grid=(rows // tile,),
        out_shape=jax.ShapeDtypeStruct((rows // 64, 8, 64, 512), jnp.bfloat16),
        in_specs=[
            pl.BlockSpec((tile, 4096), lambda i: (i, 0)),
            pl.BlockSpec((tile, 3), lambda i: (i, 0)),
            pl.BlockSpec((3, 4096, 128), lambda i: (0, 0, 0)),
            pl.BlockSpec((3, 4096, 128), lambda i: (0, 0, 0)),
            pl.BlockSpec((384, 4096), lambda i: (0, 0)),
        ],
        out_specs=pl.BlockSpec((tile // 64, 8, 64, 512), lambda i: (i, 0, 0, 0)),
        compiler_params=pltpu.CompilerParams(vmem_limit_bytes=48 * 1024 * 1024),
        cost_estimate=pl.CostEstimate(
            flops=rows * 4096 * 384 * 6, bytes_accessed=26_000_000, transcendentals=rows * 384
        ),
    )(x, mix, w_gate, w_up, w_down.reshape(384, 4096))


def on_device(
    q_latent,
    kv_cache,
    new_latent,
    cache_len,
    residual,
    w_uv,
    w_out,
    norm_gain,
    routes,
    route_weight,
    placement,
    w_gate,
    w_up,
    w_down,
):
    core = lax.axis_index("c")
    tensor = lax.axis_index("z") * 2 + lax.axis_index("xh")
    dp = (lax.axis_index("xl") * 4 + lax.axis_index("y")) * 2 + core

    slots = jnp.sum(
        jnp.where(
            routes[:, :, None] == jnp.arange(placement.shape[0], dtype=jnp.int32),
            placement,
            0,
        ),
        axis=2,
    ).astype(jnp.float32)
    plan = lax.all_gather(jnp.concatenate([slots, route_weight], axis=1), DP, axis=0, tiled=True)
    mine = (dp * 3 + jnp.arange(3)).astype(jnp.float32)
    mix = jnp.sum(
        jnp.where(plan[:, None, :8] == mine[None, :, None], plan[:, None, 8:], 0.0), axis=2
    )
    mix = mix.reshape(8, 2, 64, 3).transpose(1, 0, 2, 3).reshape(2, 512, 3)
    mix_own = lax.dynamic_index_in_dim(mix, core, 0, keepdims=False)
    mix_other = lax.dynamic_index_in_dim(mix, 1 - core, 0, keepdims=False)

    latent = attend(q_latent, kv_cache, new_latent, cache_len)
    head_latent = lax.all_to_all(latent, TN, split_axis=1, concat_axis=0, tiled=True)
    heads_out = jnp.einsum(
        "rhl,hlv->rhv", head_latent, w_uv, preferred_element_type=jnp.float32
    ).astype(jnp.bfloat16)
    projected = jnp.dot(
        heads_out.reshape(64, -1), w_out, preferred_element_type=jnp.float32
    ).astype(jnp.bfloat16)
    terms = lax.all_to_all(projected.reshape(8, 8, 4096), TN, 0, 0, tiled=True)
    attn_out = jnp.sum(terms.astype(jnp.float32), axis=0).astype(jnp.bfloat16)
    own_rows = lax.dynamic_slice_in_dim(residual, tensor * 8, 8, 0)
    hidden = (own_rows.astype(jnp.float32) + attn_out.astype(jnp.float32)).astype(jnp.bfloat16)
    hidden_f = hidden.astype(jnp.float32)
    normed = (
        hidden_f
        * lax.rsqrt(jnp.mean(hidden_f * hidden_f, axis=1, keepdims=True) + 1e-06)
        * norm_gain
    ).astype(jnp.bfloat16)

    spread = jnp.broadcast_to(normed[None], (64, 8, 4096))
    x_own = lax.all_to_all(spread, CHIPS, 0, 0, tiled=True).reshape(512, 4096)
    x_other = lax.ppermute(x_own, "c", SWAP)
    hidden_cols = lax.all_to_all(hidden.reshape(8, 8, 512), TN, 1, 0, tiled=True).reshape(64, 512)

    p_other = experts(x_other, mix_other, w_gate, w_up, w_down)
    from_other = lax.ppermute(p_other, "c", SWAP)
    p_own = experts(x_own, mix_own, w_gate, w_up, w_down)
    both = (p_own.astype(jnp.float32) + from_other.astype(jnp.float32)).astype(jnp.bfloat16)
    back = lax.all_to_all(both.reshape(64, 64, 512), CHIPS, 0, 0, tiled=True)
    mixture = jnp.sum(back.astype(jnp.float32), axis=0)
    return (hidden_cols.astype(jnp.float32) + mixture).astype(jnp.bfloat16)


def solution(mesh):
    fine = Mesh(mesh.devices.reshape(2, 4, 2, 4, 2), ("xl", "y", "c", "z", "xh"))
    both = DP + TN
    placed = (
        P(both, None, None),
        P(both, None, None),
        P(both, None),
        P(both),
        P(DP, None),
        P(TN, None, None),
        P(TN, None),
        P(),
        P(DP, None),
        P(DP, None),
        P(),
        P(DP, None, TN),
        P(DP, None, TN),
        P(DP, TN, None),
    )
    return jax.shard_map(
        on_device, mesh=fine, in_specs=placed, out_specs=P(DP, TN), check_vma=False
    )
```
